512 devices in a mesh: row: 32 (over x, y), col: 16 (over z, core).
Axes of the slice: x: 4, y: 8, z: 8, core: 2. Of those that a mesh axis runs over, the one named last changes fastest.
Arguments:
- gate_pre: bfloat16 [2048, 28672], P('col', 'row'), may hold values from -6 to 6
- up_pre: bfloat16 [2048, 28672], P('col', 'row'), may hold values from -6 to 6
- down_weight: bfloat16 [28672, 4096], P('row', 'col'), may hold values from -0.03125 to 0.03125
- out_grad: bfloat16 [2048, 4096], P('col', 'row'), may hold values from -6 to 6
Outputs:
- output: bfloat16 [2048, 4096], P('col', 'row')
- gate_grad: bfloat16 [2048, 28672], P('col', 'row')
- up_grad: bfloat16 [2048, 28672], P('col', 'row')
- weight_grad: bfloat16 [28672, 4096], P('row', 'col')
The draws below stay inside these ranges and needn't reach their ends.
All inputs are finite; a program needn't handle non-finite values.
Results may differ from the reference program's by a relative error of at most 0.0049.
Values may be sent and summed in bfloat16 or wider, within the bound.
No kernel may reach another device: no remote copies, remote signals or barrier semaphores. Data moves between devices by JAX's collectives and lax.ppermute only.
A program may use at most 64 MiB of HBM per device.

```python
import jax
import jax.numpy as jnp

D = 4096
FF = 28672
TOKENS = 2048


def level_of(stream_key, shape, cuts, least, top_value):
    loudness = 1.0
    for dim, parts in cuts:
        heights = jax.random.uniform(jax.random.fold_in(jax.random.fold_in(stream_key, 6), dim), (parts,), jnp.float32, least / len(cuts), top_value / len(cuts))
        loudness = loudness * jnp.repeat(jnp.exp(heights), shape[dim] // parts).reshape((-1,) + (1,) * (len(shape) - 1 - dim))
    return loudness


def noise(key, shape, spread, reach, pieces=(), kind=jnp.bfloat16):
    entries = jax.random.normal(key, shape, jnp.float32) * spread
    if len(pieces) > 0:
        entries = level_of(key, shape, pieces, -0.22, 0.18) * entries
    return jnp.clip(entries, min=-reach, max=reach).astype(kind)


def setup_inputs(seed: int = 0) -> dict:
    arg_keys = jax.random.split(jax.random.key(seed), 5)
    return {
        "gate_pre": noise(arg_keys[0], (TOKENS, FF), 1.0, 6.0, ((0, 16), (1, 32))),
        "up_pre": noise(arg_keys[1], (TOKENS, FF), 1.0, 6.0, ((0, 16), (1, 32))),
        "down_weight": noise(arg_keys[2], (FF, D), FF ** -0.5, 0.03125, ((0, 32), (1, 16))),
        "out_grad": noise(arg_keys[3], (TOKENS, D), 1.0, 6.0, ((0, 16), (1, 32))),
    }


def reference(gate_pre, up_pre, down_weight, out_grad):
    gate_value = gate_pre.astype(jnp.float32)
    up_value = up_pre.astype(jnp.float32)
    sigmoid_gate = jax.nn.sigmoid(gate_value)
    hidden = (gate_value * sigmoid_gate * up_value).astype(jnp.bfloat16)
    output = jnp.dot(hidden, down_weight, preferred_element_type=jnp.float32).astype(jnp.bfloat16)
    hidden_grad = jnp.dot(out_grad, down_weight.T, preferred_element_type=jnp.float32)
    gate_grad = hidden_grad * up_value * sigmoid_gate * (1.0 + gate_value * (1.0 - sigmoid_gate))
    up_grad = hidden_grad * gate_value * sigmoid_gate
    weight_grad = jnp.dot(hidden.T, out_grad, preferred_element_type=jnp.float32)
    return (output, gate_grad.astype(jnp.bfloat16), up_grad.astype(jnp.bfloat16), weight_grad.astype(jnp.bfloat16))
```

```python
import jax
import jax.numpy as jnp
from jax import lax
from jax.experimental import pallas as pl
from jax.experimental.pallas import tpu as pltpu
from jax.sharding import Mesh, PartitionSpec as P

X, Y, Z, CORES = 4, 8, 8, 2
AXES = ("x", "y", "z", "core")
WHOLE = pl.BlockSpec(memory_space=pltpu.VMEM)
UNREAD = pl.BlockSpec(memory_space=pl.ANY)


def index_of(x, y, z, core):
    return ((x * Y + y) * Z + z) * CORES + core


def to_feature_owner():
    pairs = []
    for x in range(X):
        for y in range(Y):
            for z in range(Z):
                for core in range(CORES):
                    target = index_of((y % 4 + 2 * core) % 4, z, 2 * x + y // 4, core)
                    pairs.append((index_of(x, y, z, core), target))
    return pairs


def kernel_call(kernel, out_shape, in_specs, flops, size):
    return pl.pallas_call(
        kernel,
        out_shape=out_shape,
        in_specs=in_specs,
        out_specs=jax.tree.map(lambda _: WHOLE, out_shape),
        compiler_params=pltpu.CompilerParams(vmem_limit_bytes=40 * 1024 * 1024),
        cost_estimate=pl.CostEstimate(flops=flops, bytes_accessed=size, transcendentals=0),
    )


def hidden_kernel(gate_ref, up_ref, grad_ref, hidden_ref, grad_out_ref):
    gate = gate_ref[...].astype(jnp.float32)
    up = up_ref[...].astype(jnp.float32)
    hidden_ref[...] = (gate * jax.nn.sigmoid(gate) * up).astype(jnp.bfloat16)
    grad_out_ref[...] = grad_ref[...]


def share_kernel(grad_ref, own_ref, other_ref, _, share_ref):
    sub = grad_ref.shape[2]
    total = None
    for q in range(grad_ref.shape[0]):
        weights = (own_ref if q < 2 else other_ref)[:, (q % 2) * sub : (q % 2 + 1) * sub]
        term = lax.dot_general(grad_ref[q], weights, (((1,), (1,)), ((), ())), preferred_element_type=jnp.float32)
        total = term if total is None else total + term
    share_ref[...] = total.astype(jnp.bfloat16)


def output_kernel(hidden_ref, own_ref, other_ref, out_ref):
    sub = out_ref.shape[2]
    for half, weights in enumerate((own_ref, other_ref)):
        product = jnp.dot(hidden_ref[...], weights[...], preferred_element_type=jnp.float32).astype(jnp.bfloat16)
        out_ref[2 * half] = product[:, :sub]
        out_ref[2 * half + 1] = product[:, sub:]


def weight_grad_kernel(hidden_ref, grad_ref, _, own_ref, other_ref):
    sub = grad_ref.shape[2]
    for q in range(grad_ref.shape[0]):
        target = own_ref if q < 2 else other_ref
        target[:, (q % 2) * sub : (q % 2 + 1) * sub] = lax.dot_general(
            hidden_ref[...], grad_ref[q], (((0,), (0,)), ((), ())), preferred_element_type=jnp.float32
        )


def sum_kernel(parts_ref, sum_ref):
    total = parts_ref[0].astype(jnp.float32)
    for i in range(1, parts_ref.shape[0]):
        total = total + parts_ref[i].astype(jnp.float32)
    sum_ref[...] = total.astype(jnp.bfloat16)


def add_kernel(a_ref, b_ref, sum_ref):
    sum_ref[...] = (a_ref[...] + b_ref[...]).astype(jnp.bfloat16)


def gradient_kernel(hidden_grad_ref, gate_ref, up_ref, gate_grad_ref, up_grad_ref):
    hidden_grad = hidden_grad_ref[...].astype(jnp.float32)
    gate = gate_ref[...].astype(jnp.float32)
    up = up_ref[...].astype(jnp.float32)
    sigmoid = jax.nn.sigmoid(gate)
    gate_grad_ref[...] = (hidden_grad * up * sigmoid * (1.0 + gate * (1.0 - sigmoid))).astype(jnp.bfloat16)
    up_grad_ref[...] = (hidden_grad * gate * sigmoid).astype(jnp.bfloat16)


def body(gate_pre, up_pre, down_weight, out_grad):
    bf16, f32, shape = jnp.bfloat16, jnp.float32, jax.ShapeDtypeStruct
    there = to_feature_owner()
    back = [(b, a) for a, b in there]
    tokens, units = gate_pre.shape
    sub, features = out_grad.shape[1], down_weight.shape[1]
    rows = Z * tokens
    flops = 2 * rows * units * CORES * features
    swap = [(0, 1), (1, 0)]

    hidden, grad = kernel_call(
        hidden_kernel, (shape((tokens, units), bf16), shape(out_grad.shape, bf16)), [WHOLE] * 3, 0, 6 * tokens * units
    )(gate_pre, up_pre, out_grad)
    hidden_all = lax.all_gather(hidden, "z", axis=0, tiled=True)
    other_weight = lax.ppermute(down_weight, "core", swap)

    grad = lax.ppermute(grad, AXES, there)
    grad = lax.all_to_all(jnp.broadcast_to(grad, (Y, tokens, sub)), "y", split_axis=0, concat_axis=0, tiled=True)
    grad = jnp.broadcast_to(grad.reshape(rows, sub), (X, rows, sub))
    grad = lax.all_to_all(grad, "x", split_axis=0, concat_axis=0, tiled=True)

    share = kernel_call(
        share_kernel, shape((rows, units), bf16), [WHOLE, WHOLE, WHOLE, UNREAD], flops, 4 * rows * units
    )(grad, down_weight, other_weight, hidden_all)
    hidden_grad = lax.psum_scatter(share, "z", scatter_dimension=0, tiled=True)
    gate_grad, up_grad = kernel_call(
        gradient_kernel, (shape((tokens, units), bf16),) * 2, [WHOLE] * 3, 0, 10 * tokens * units
    )(hidden_grad, gate_pre, up_pre)

    output = kernel_call(output_kernel, shape((X, rows, sub), bf16), [WHOLE] * 3, flops, 4 * rows * units)(
        hidden_all, down_weight, other_weight
    )
    output = lax.all_to_all(output, "x", split_axis=0, concat_axis=0, tiled=True)
    output = kernel_call(sum_kernel, shape((rows, sub), bf16), [WHOLE], 0, 10 * rows * sub)(output)
    output = lax.all_to_all(output.reshape(Y, tokens, sub), "y", split_axis=0, concat_axis=0, tiled=True)
    output_sum = kernel_call(sum_kernel, shape((tokens, sub), bf16), [WHOLE], 0, 18 * tokens * sub)(output)
    output = lax.ppermute(output_sum, AXES, back)

    own, other = kernel_call(
        weight_grad_kernel, (shape((units, features), f32),) * 2, [WHOLE, WHOLE, UNREAD], flops, 4 * rows * units
    )(hidden_all, grad, output_sum)
    weight_grad = kernel_call(add_kernel, shape((units, features), bf16), [WHOLE] * 2, 0, 10 * units * features)(
        own, lax.ppermute(other, "core", swap)
    )
    return output, gate_grad, up_grad, weight_grad


def solution(mesh):
    chips = Mesh(mesh.devices.reshape(X, Y, Z, CORES), AXES)
    by_token = P(("z", "core"), ("x", "y"))
    by_unit = P(("x", "y"), ("z", "core"))
    return jax.shard_map(
        body,
        mesh=chips,
        in_specs=(by_token, by_token, by_unit, by_token),
        out_specs=(by_token, by_token, by_token, by_unit),
        check_vma=False,
    )
```

```python
import jax
import jax.numpy as jnp
from jax import lax
from jax.experimental import pallas as pl
from jax.experimental.pallas import tpu as pltpu
from jax.sharding import Mesh, PartitionSpec as P

X, Y, Z, CORES = 4, 8, 8, 2
AXES = ("x", "y", "z", "core")
def index_of(x, y, z, core):
    return ((x * Y + y) * Z + z) * CORES + core


def to_feature_owner():
    pairs = []
    for x in range(X):
        for y in range(Y):
            for z in range(Z):
                for core in range(CORES):
                    target = index_of((y % 4 + 2 * core) % 4, z, 2 * x + y // 4, core)
                    pairs.append((index_of(x, y, z, core), target))
    return pairs


def kernel_call(kernel, out_shape, flops, size, vmem=24, **more):
    return pl.pallas_call(
        kernel,
        out_shape=out_shape,
        compiler_params=pltpu.CompilerParams(vmem_limit_bytes=vmem * 1024 * 1024),
        cost_estimate=pl.CostEstimate(flops=flops, bytes_accessed=size, transcendentals=0),
        **more,
    )


def streamed_call(kernel, out_shape, flops, size, scratch_shapes):
    in_hbm = pl.BlockSpec(memory_space=pl.ANY)

    def call(*arrays):
        return kernel_call(
            kernel,
            out_shape,
            flops,
            size,
            vmem=60,
            in_specs=[in_hbm] * len(arrays),
            out_specs=jax.tree.map(lambda _: in_hbm, out_shape),
            scratch_shapes=scratch_shapes,
        )(*arrays)

    return call


def started(source, target, sem):
    copy = pltpu.make_async_copy(source, target, sem)
    copy.start()
    return copy


def hidden_kernel(gate_ref, up_ref, hidden_ref, gate_in, up_in, hidden_out, sems):
    copies = [started(gate_ref, gate_in, sems.at[0]), started(up_ref, up_in, sems.at[1])]
    for copy in copies:
        copy.wait()
    gate = gate_in[...].astype(jnp.float32)
    up = up_in[...].astype(jnp.float32)
    hidden_out[...] = (gate * jax.nn.sigmoid(gate) * up).astype(jnp.bfloat16)
    started(hidden_out, hidden_ref, sems.at[2]).wait()


def share_kernel(grad_ref, own_ref, other_ref, share_ref, mine_ref):
    z_blocks, tokens, _ = share_ref.shape
    weights = jnp.concatenate([own_ref[...], other_ref[...]], axis=1)

    def product(grad):
        return lax.dot_general(grad, weights, (((1,), (1,)), ((), ())), preferred_element_type=jnp.float32)

    grad = jnp.concatenate([grad_ref[q].reshape(z_blocks * tokens, -1) for q in range(X)], axis=1)
    share_ref[...] = product(grad).astype(jnp.bfloat16).reshape(share_ref.shape)
    here = lax.axis_index("z")
    share_ref[here] = jnp.zeros(mine_ref.shape, jnp.bfloat16)
    mine_ref[...] = product(jnp.concatenate([grad_ref[q, here] for q in range(X)], axis=1))


def output_kernel(hidden_ref, own_ref, other_ref, out_ref):
    _, z_blocks, tokens, sub = out_ref.shape
    for half, weights in enumerate((own_ref, other_ref)):
        product = jnp.dot(hidden_ref[...], weights[...], preferred_element_type=jnp.float32).astype(jnp.bfloat16)
        for h in range(2):
            out_ref[2 * half + h] = product[:, h * sub : (h + 1) * sub].reshape(z_blocks, tokens, sub)


def weight_grad_kernel(hidden_ref, grad_ref, own_ref, other_ref):
    rows = hidden_ref.shape[0]
    for half, out_ref in enumerate((own_ref, other_ref)):
        grad = jnp.concatenate([grad_ref[2 * half + h].reshape(rows, -1) for h in range(2)], axis=1)
        out_ref[...] = lax.dot_general(
            hidden_ref[...], grad, (((0,), (0,)), ((), ())), preferred_element_type=jnp.float32
        ).astype(out_ref.dtype)


def sum_kernel(parts_ref, sum_ref):
    total = parts_ref[0].astype(jnp.float32)
    for i in range(1, parts_ref.shape[0]):
        total = total + parts_ref[i].astype(jnp.float32)
    sum_ref[...] = total.astype(jnp.bfloat16)


def add_kernel(a_ref, b_ref, sum_ref):
    sum_ref[...] = (a_ref[...] + b_ref[...]).astype(jnp.bfloat16)


def gradient_kernel(mine_ref, others_ref, gate_ref, up_ref, gate_grad_ref, up_grad_ref):
    hidden_grad = mine_ref[...] + others_ref[...].astype(jnp.float32)
    gate = gate_ref[...].astype(jnp.float32)
    up = up_ref[...].astype(jnp.float32)
    sigmoid = jax.nn.sigmoid(gate)
    gate_grad_ref[...] = (hidden_grad * up * sigmoid * (1.0 + gate * (1.0 - sigmoid))).astype(jnp.bfloat16)
    up_grad_ref[...] = (hidden_grad * gate * sigmoid).astype(jnp.bfloat16)


def body(gate_pre, up_pre, down_weight, out_grad):
    bf16, f32, shape = jnp.bfloat16, jnp.float32, jax.ShapeDtypeStruct
    there = to_feature_owner()
    back = [(b, a) for a, b in there]
    tokens, units = gate_pre.shape
    sub, features = out_grad.shape[1], down_weight.shape[1]
    rows = Z * tokens
    flops = 2 * rows * units * CORES * features
    swap = [(0, 1), (1, 0)]
    together = lax.optimization_barrier

    def exchanged(array, axis):
        return lax.all_to_all(array, axis, split_axis=0, concat_axis=0, tiled=True)

    block = (tokens, units)
    vmem, dma = pltpu.VMEM, pltpu.SemaphoreType.DMA
    hidden = streamed_call(
        hidden_kernel, shape(block, bf16), 0, 6 * tokens * units, [vmem(block, bf16)] * 3 + [dma((3,))]
    )(gate_pre, up_pre)
    hidden, out_grad = together((hidden, out_grad))
    hidden_all = lax.all_gather(hidden, "z", axis=0, tiled=True)

    grad = lax.ppermute(out_grad, AXES, there)
    other_weight = lax.ppermute(down_weight, "core", swap)
    grad = exchanged(jnp.broadcast_to(grad, (Y, tokens, sub)), "y")
    grad = exchanged(jnp.broadcast_to(grad, (X, Y, tokens, sub)), "x")

    output = kernel_call(output_kernel, shape((X, Y, tokens, sub), bf16), flops, 4 * rows * units)(
        hidden_all, down_weight, other_weight
    )
    output, grad = together((output, grad))

    share, mine = kernel_call(
        share_kernel, (shape((Z, tokens, units), bf16), shape(block, f32)), flops, 4 * rows * units
    )(grad, down_weight, other_weight)
    others = lax.psum_scatter(share.reshape(rows, units), "z", scatter_dimension=0, tiled=True)
    gate_grad, up_grad = kernel_call(gradient_kernel, (shape(block, bf16),) * 2, 0, 14 * tokens * units)(
        mine, others, gate_pre, up_pre
    )

    output = exchanged(output, "x")
    output = kernel_call(sum_kernel, shape((Y, tokens, sub), bf16), 0, 10 * rows * sub)(output)
    output = exchanged(output, "y")
    output = kernel_call(sum_kernel, shape((tokens, sub), bf16), 0, 18 * tokens * sub)(output)
    output = lax.ppermute(output, AXES, back)
    output, gate_grad, up_grad = together((output, gate_grad, up_grad))

    own, other = kernel_call(
        weight_grad_kernel, (shape((units, features), f32),) * 2, flops, 4 * rows * units
    )(hidden_all, grad)
    weight_grad = kernel_call(add_kernel, shape((units, features), bf16), 0, 10 * units * features)(
        own, lax.ppermute(other, "core", swap)
    )
    return output, gate_grad, up_grad, weight_grad


def solution(mesh):
    chips = Mesh(mesh.devices.reshape(X, Y, Z, CORES), AXES)
    by_token = P(("z", "core"), ("x", "y"))
    by_unit = P(("x", "y"), ("z", "core"))
    return jax.shard_map(
        body,
        mesh=chips,
        in_specs=(by_token, by_token, by_unit, by_token),
        out_specs=(by_token, by_token, by_token, by_unit),
        check_vma=False,
    )
```

```python
import jax
import jax.numpy as jnp
import numpy as np
from jax import lax
from jax.experimental import pallas as pl
from jax.experimental.pallas import tpu as pltpu
from jax.sharding import Mesh, PartitionSpec as P

X, Y, Z, CORES = 4, 8, 8, 2
SIDES = 2
AXES = ("x", "step", "side", "z", "core")


def index_of(x, y, z, core):
    return ((x * Y + y) * Z + z) * CORES + core


def place(z, tokens, q):
    ahead = lax.rem(tokens - z + Z, Z)
    even = lax.rem(ahead, 2) == 0
    turn = jnp.where(ahead >= 4, jnp.where(even, 0, 3), jnp.where(even, 2, 1))
    first = 4 * lax.rem(z, 2)
    y = jnp.where((ahead < 2) | (ahead > 5), lax.rem(first + 7 - q, Y), first + q)
    return lax.rem(z // 2 + turn, X), y


def to_feature_owner():
    x, y, z, core = (a.ravel() for a in np.indices((X, Y, Z, CORES)))
    plane = 2 * x + y // 4
    ahead = (z - plane) % Z
    turn = np.array([2, 1, 2, 1, 0, 3, 0, 3])[ahead]
    target_y = np.where((ahead < 2) | (ahead > 5), (4 * (plane % 2) + 7 - y % 4) % Y, y)
    targets = index_of((plane // 2 + turn) % X, target_y, plane, core)
    return [(int(a), int(b)) for a, b in zip(index_of(x, y, z, core), targets)]


def slot(tokens, half, h):
    core = lax.axis_index("core")
    q = 2 * (core if half == 0 else 1 - core) + h
    x, y = place(lax.axis_index("z"), tokens, q)
    return x * SIDES + lax.rem(y, SIDES), y // SIDES


def grad_of(grad_ref, tokens, half):
    blocks = [jnp.concatenate([grad_ref[slot(t, half, h)] for h in range(2)], axis=1) for t in tokens]
    return jnp.concatenate(blocks, axis=0)


def kernel_call(kernel, out_shape, flops, size, vmem=24, **more):
    return pl.pallas_call(
        kernel,
        out_shape=out_shape,
        compiler_params=pltpu.CompilerParams(vmem_limit_bytes=vmem * 1024 * 1024),
        cost_estimate=pl.CostEstimate(flops=flops, bytes_accessed=size, transcendentals=0),
        **more,
    )


def streamed_call(kernel, out_shape, flops, size, scratch_shapes):
    in_hbm = pl.BlockSpec(memory_space=pl.ANY)

    def call(*arrays):
        return kernel_call(
            kernel,
            out_shape,
            flops,
            size,
            vmem=60,
            in_specs=[in_hbm] * len(arrays),
            out_specs=jax.tree.map(lambda _: in_hbm, out_shape),
            scratch_shapes=scratch_shapes,
        )(*arrays)

    return call


def started(source, target, sem):
    copy = pltpu.make_async_copy(source, target, sem)
    copy.start()
    return copy


def hidden_kernel(gate_ref, up_ref, hidden_ref, gate_in, up_in, hidden_out, sems):
    copies = [started(gate_ref, gate_in, sems.at[0]), started(up_ref, up_in, sems.at[1])]
    for copy in copies:
        copy.wait()
    gate = gate_in[...].astype(jnp.float32)
    up = up_in[...].astype(jnp.float32)
    hidden_out[...] = (gate * jax.nn.sigmoid(gate) * up).astype(jnp.bfloat16)
    started(hidden_out, hidden_ref, sems.at[2]).wait()


def share_kernel(grad_ref, own_ref, other_ref, share_ref, mine_ref):
    weights = jnp.concatenate([own_ref[...], other_ref[...]], axis=1)

    def product(tokens):
        grad = jnp.concatenate([grad_of(grad_ref, tokens, half) for half in range(2)], axis=1)
        return lax.dot_general(grad, weights, (((1,), (1,)), ((), ())), preferred_element_type=jnp.float32)

    share_ref[...] = product(range(Z)).astype(jnp.bfloat16).reshape(share_ref.shape)
    here = lax.axis_index("z")
    share_ref[here] = jnp.zeros(mine_ref.shape, jnp.bfloat16)
    mine_ref[...] = product([here])


def output_kernel(hidden_ref, own_ref, other_ref, out_ref):
    _, _, tokens, sub = out_ref.shape
    for half, weights in enumerate((own_ref, other_ref)):
        product = jnp.dot(hidden_ref[...], weights[...], preferred_element_type=jnp.float32).astype(jnp.bfloat16)
        for z in range(Z):
            for h in range(2):
                out_ref[slot(z, half, h)] = product[z * tokens : (z + 1) * tokens, h * sub : (h + 1) * sub]


def weight_grad_kernel(hidden_ref, grad_ref, own_ref, other_ref):
    for half, out_ref in enumerate((own_ref, other_ref)):
        out_ref[...] = lax.dot_general(
            hidden_ref[...],
            grad_of(grad_ref, range(Z), half),
            (((0,), (0,)), ((), ())),
            preferred_element_type=jnp.float32,
        ).astype(out_ref.dtype)


def sum_kernel(parts_ref, sum_ref):
    total = parts_ref[0].astype(jnp.float32)
    for i in range(1, parts_ref.shape[0]):
        total = total + parts_ref[i].astype(jnp.float32)
    sum_ref[...] = total.astype(jnp.bfloat16)


def add_kernel(a_ref, b_ref, sum_ref):
    sum_ref[...] = (a_ref[...] + b_ref[...]).astype(jnp.bfloat16)


def gradient_kernel(mine_ref, others_ref, gate_ref, up_ref, gate_grad_ref, up_grad_ref):
    hidden_grad = mine_ref[...] + others_ref[...].astype(jnp.float32)
    gate = gate_ref[...].astype(jnp.float32)
    up = up_ref[...].astype(jnp.float32)
    sigmoid = jax.nn.sigmoid(gate)
    gate_grad_ref[...] = (hidden_grad * up * sigmoid * (1.0 + gate * (1.0 - sigmoid))).astype(jnp.bfloat16)
    up_grad_ref[...] = (hidden_grad * gate * sigmoid).astype(jnp.bfloat16)


def body(gate_pre, up_pre, down_weight, out_grad):
    bf16, f32, shape = jnp.bfloat16, jnp.float32, jax.ShapeDtypeStruct
    there = to_feature_owner()
    back = [(b, a) for a, b in there]
    tokens, units = gate_pre.shape
    sub, features = out_grad.shape[1], down_weight.shape[1]
    rows = Z * tokens
    flops = 2 * rows * units * CORES * features
    swap = [(0, 1), (1, 0)]
    together = lax.optimization_barrier

    def exchanged(array, axis):
        return lax.all_to_all(array, axis, split_axis=0, concat_axis=0, tiled=True)

    block = (tokens, units)
    vmem, dma = pltpu.VMEM, pltpu.SemaphoreType.DMA
    hidden = streamed_call(
        hidden_kernel, shape(block, bf16), 0, 6 * tokens * units, [vmem(block, bf16)] * 3 + [dma((3,))]
    )(gate_pre, up_pre)
    hidden, out_grad = together((hidden, out_grad))
    hidden_all = lax.all_gather(hidden, "z", axis=0, tiled=True)

    grad = lax.ppermute(out_grad, AXES, there)
    other_weight = lax.ppermute(down_weight, "core", swap)
    steps = Y // SIDES
    grad = exchanged(jnp.broadcast_to(grad, (steps, tokens, sub)), "step")
    grad = exchanged(jnp.broadcast_to(grad, (X * SIDES, steps, tokens, sub)), ("x", "side"))

    share, mine = kernel_call(
        share_kernel, (shape((Z, tokens, units), bf16), shape(block, f32)), flops, 4 * rows * units
    )(grad, down_weight, other_weight)
    hidden_all, share = together((hidden_all, share))
    output = kernel_call(output_kernel, shape((X * SIDES, steps, tokens, sub), bf16), flops, 4 * rows * units)(
        hidden_all, down_weight, other_weight
    )

    others = lax.psum_scatter(share.reshape(rows, units), "z", scatter_dimension=0, tiled=True)
    gate_grad, up_grad = kernel_call(gradient_kernel, (shape(block, bf16),) * 2, 0, 14 * tokens * units)(
        mine, others, gate_pre, up_pre
    )

    output = exchanged(output, ("x", "side"))
    output = kernel_call(sum_kernel, shape((steps, tokens, sub), bf16), 0, 10 * rows * sub)(output)
    output = exchanged(output, "step")
    output = kernel_call(sum_kernel, shape((tokens, sub), bf16), 0, 10 * tokens * sub)(output)
    output = lax.ppermute(output, AXES, back)
    output, gate_grad, up_grad = together((output, gate_grad, up_grad))

    own, other = kernel_call(
        weight_grad_kernel, (shape((units, features), f32),) * 2, flops, 4 * rows * units
    )(hidden_all, grad)
    weight_grad = kernel_call(add_kernel, shape((units, features), bf16), 0, 10 * units * features)(
        own, lax.ppermute(other, "core", swap)
    )
    return output, gate_grad, up_grad, weight_grad


def solution(mesh):
    chips = Mesh(mesh.devices.reshape(X, Y // SIDES, SIDES, Z, CORES), AXES)
    by_token = P(("z", "core"), ("x", "step", "side"))
    by_unit = P(("x", "step", "side"), ("z", "core"))
    return jax.shard_map(
        body,
        mesh=chips,
        in_specs=(by_token, by_token, by_unit, by_token),
        out_specs=(by_token, by_token, by_token, by_unit),
        check_vma=False,
    )
```

```python
import jax
import jax.numpy as jnp
import numpy as np
from jax import lax
from jax.experimental import pallas as pl
from jax.experimental.pallas import tpu as pltpu
from jax.sharding import Mesh, PartitionSpec as P

X, Y, Z, CORES = 4, 8, 8, 2
SIDES = 2
AXES = ("x", "step", "side", "z", "core")


def index_of(x, y, z, core):
    return ((x * Y + y) * Z + z) * CORES + core


def place(z, tokens, q):
    ahead = lax.rem(tokens - z + Z, Z)
    even = lax.rem(ahead, 2) == 0
    turn = jnp.where(ahead >= 4, jnp.where(even, 0, 3), jnp.where(even, 2, 1))
    first = 4 * lax.rem(z, 2)
    y = jnp.where((ahead < 2) | (ahead > 5), lax.rem(first + 7 - q, Y), first + q)
    return lax.rem(z // 2 + turn, X), y


def to_feature_owner():
    x, y, z, core = (a.ravel() for a in np.indices((X, Y, Z, CORES)))
    plane = 2 * x + y // 4
    ahead = (z - plane) % Z
    turn = np.array([2, 1, 2, 1, 0, 3, 0, 3])[ahead]
    target_y = np.where((ahead < 2) | (ahead > 5), (4 * (plane % 2) + 7 - y % 4) % Y, y)
    targets = index_of((plane // 2 + turn) % X, target_y, plane, core)
    return [(int(a), int(b)) for a, b in zip(index_of(x, y, z, core), targets)]


def slot(tokens, half, h):
    core = lax.axis_index("core")
    q = 2 * (core if half == 0 else 1 - core) + h
    x, y = place(lax.axis_index("z"), tokens, q)
    return x * SIDES + lax.rem(y, SIDES), y // SIDES


def grad_of(grad_ref, tokens, half):
    blocks = [jnp.concatenate([grad_ref[slot(t, half, h)] for h in range(2)], axis=1) for t in tokens]
    return jnp.concatenate(blocks, axis=0)


def kernel_call(kernel, out_shape, flops, size, vmem=24, **more):
    return pl.pallas_call(
        kernel,
        out_shape=out_shape,
        compiler_params=pltpu.CompilerParams(vmem_limit_bytes=vmem * 1024 * 1024),
        cost_estimate=pl.CostEstimate(flops=flops, bytes_accessed=size, transcendentals=0),
        **more,
    )


def streamed_call(kernel, out_shape, flops, size, scratch_shapes):
    in_hbm = pl.BlockSpec(memory_space=pl.ANY)

    def call(*arrays):
        return kernel_call(
            kernel,
            out_shape,
            flops,
            size,
            vmem=60,
            in_specs=[in_hbm] * len(arrays),
            out_specs=jax.tree.map(lambda _: in_hbm, out_shape),
            scratch_shapes=scratch_shapes,
        )(*arrays)

    return call


def started(source, target, sem):
    copy = pltpu.make_async_copy(source, target, sem)
    copy.start()
    return copy


def hidden_kernel(gate_ref, up_ref, hidden_ref, gate_in, up_in, hidden_out, sems):
    parts = 2
    rows = gate_ref.shape[0] // parts
    spans = [pl.ds(i * rows, rows) for i in range(parts)]
    copies = [
        (started(gate_ref.at[r], gate_in.at[r], sems.at[2 * i]), started(up_ref.at[r], up_in.at[r], sems.at[2 * i + 1]))
        for i, r in enumerate(spans)
    ]
    stores = []
    for i, r in enumerate(spans):
        for copy in copies[i]:
            copy.wait()
        gate = gate_in[r].astype(jnp.float32)
        up = up_in[r].astype(jnp.float32)
        hidden_out[r] = (gate * jax.nn.sigmoid(gate) * up).astype(jnp.bfloat16)
        stores.append(started(hidden_out.at[r], hidden_ref.at[r], sems.at[2 * parts + i]))
    for store in stores:
        store.wait()


def share_kernel(grad_ref, own_ref, other_ref, share_ref, mine_ref):
    weights = jnp.concatenate([own_ref[...], other_ref[...]], axis=1)

    def product(tokens):
        grad = jnp.concatenate([grad_of(grad_ref, tokens, half) for half in range(2)], axis=1)
        return lax.dot_general(grad, weights, (((1,), (1,)), ((), ())), preferred_element_type=jnp.float32)

    share_ref[...] = product(range(Z)).astype(jnp.bfloat16).reshape(share_ref.shape)
    here = lax.axis_index("z")
    share_ref[here] = jnp.zeros(mine_ref.shape, jnp.bfloat16)
    mine_ref[...] = product([here])


def output_kernel(hidden_ref, own_ref, other_ref, out_ref):
    _, _, tokens, sub = out_ref.shape
    for half, weights in enumerate((own_ref, other_ref)):
        product = jnp.dot(hidden_ref[...], weights[...], preferred_element_type=jnp.float32).astype(jnp.bfloat16)
        for z in range(Z):
            for h in range(2):
                out_ref[slot(z, half, h)] = product[z * tokens : (z + 1) * tokens, h * sub : (h + 1) * sub]


def weight_grad_kernel(hidden_ref, grad_ref, own_ref, other_ref):
    for half, out_ref in enumerate((own_ref, other_ref)):
        out_ref[...] = lax.dot_general(
            hidden_ref[...],
            grad_of(grad_ref, range(Z), half),
            (((0,), (0,)), ((), ())),
            preferred_element_type=jnp.float32,
        ).astype(out_ref.dtype)


def sum_kernel(parts_ref, sum_ref):
    total = parts_ref[0].astype(jnp.float32)
    for i in range(1, parts_ref.shape[0]):
        total = total + parts_ref[i].astype(jnp.float32)
    sum_ref[...] = total.astype(jnp.bfloat16)


def add_kernel(a_ref, b_ref, sum_ref):
    sum_ref[...] = (a_ref[...] + b_ref[...]).astype(jnp.bfloat16)


def gradient_kernel(mine_ref, others_ref, gate_ref, up_ref, gate_grad_ref, up_grad_ref):
    hidden_grad = mine_ref[...] + others_ref[...].astype(jnp.float32)
    gate = gate_ref[...].astype(jnp.float32)
    up = up_ref[...].astype(jnp.float32)
    sigmoid = jax.nn.sigmoid(gate)
    gate_grad_ref[...] = (hidden_grad * up * sigmoid * (1.0 + gate * (1.0 - sigmoid))).astype(jnp.bfloat16)
    up_grad_ref[...] = (hidden_grad * gate * sigmoid).astype(jnp.bfloat16)


def body(gate_pre, up_pre, down_weight, out_grad):
    bf16, f32, shape = jnp.bfloat16, jnp.float32, jax.ShapeDtypeStruct
    there = to_feature_owner()
    back = [(b, a) for a, b in there]
    tokens, units = gate_pre.shape
    sub, features = out_grad.shape[1], down_weight.shape[1]
    rows = Z * tokens
    flops = 2 * rows * units * CORES * features
    swap = [(0, 1), (1, 0)]
    together = lax.optimization_barrier

    def exchanged(array, axis):
        return lax.all_to_all(array, axis, split_axis=0, concat_axis=0, tiled=True)

    block = (tokens, units)
    vmem, dma = pltpu.VMEM, pltpu.SemaphoreType.DMA
    hidden = streamed_call(
        hidden_kernel, shape(block, bf16), 0, 6 * tokens * units, [vmem(block, bf16)] * 3 + [dma((6,))]
    )(gate_pre, up_pre)
    hidden, out_grad = together((hidden, out_grad))
    hidden_all = lax.all_gather(hidden, "z", axis=0, tiled=True)

    grad = lax.ppermute(out_grad, AXES, there)
    other_weight = lax.ppermute(down_weight, "core", swap)
    steps = Y // SIDES
    grad = exchanged(jnp.broadcast_to(grad, (steps, tokens, sub)), "step")
    grad = exchanged(jnp.broadcast_to(grad, (X * SIDES, steps, tokens, sub)), ("x", "side"))

    share, mine = kernel_call(
        share_kernel, (shape((Z, tokens, units), bf16), shape(block, f32)), flops, 4 * rows * units
    )(grad, down_weight, other_weight)
    hidden_all, _ = together((hidden_all, mine))
    output = kernel_call(output_kernel, shape((X * SIDES, steps, tokens, sub), bf16), flops, 4 * rows * units)(
        hidden_all, down_weight, other_weight
    )

    others = lax.psum_scatter(share.reshape(rows, units), "z", scatter_dimension=0, tiled=True)
    gate_grad, up_grad = kernel_call(gradient_kernel, (shape(block, bf16),) * 2, 0, 14 * tokens * units)(
        mine, others, gate_pre, up_pre
    )

    output = exchanged(output, ("x", "side"))
    output = kernel_call(sum_kernel, shape((steps, tokens, sub), bf16), 0, 10 * rows * sub)(output)
    output = exchanged(output, "step")
    output = kernel_call(sum_kernel, shape((tokens, sub), bf16), 0, 10 * tokens * sub)(output)
    output = lax.ppermute(output, AXES, back)
    output, gate_grad, up_grad = together((output, gate_grad, up_grad))

    own, other = kernel_call(
        weight_grad_kernel, (shape((units, features), f32),) * 2, flops, 4 * rows * units
    )(hidden_all, grad)
    weight_grad = kernel_call(add_kernel, shape((units, features), bf16), 0, 10 * units * features)(
        own, lax.ppermute(other, "core", swap)
    )
    return output, gate_grad, up_grad, weight_grad


def solution(mesh):
    chips = Mesh(mesh.devices.reshape(X, Y // SIDES, SIDES, Z, CORES), AXES)
    by_token = P(("z", "core"), ("x", "step", "side"))
    by_unit = P(("x", "step", "side"), ("z", "core"))
    return jax.shard_map(
        body,
        mesh=chips,
        in_specs=(by_token, by_token, by_unit, by_token),
        out_specs=(by_token, by_token, by_token, by_unit),
        check_vma=False,
    )
```

```python
import jax
import jax.numpy as jnp
import numpy as np
from jax import lax
from jax.experimental import pallas as pl
from jax.experimental.pallas import tpu as pltpu
from jax.sharding import Mesh, PartitionSpec as P

X, Y, Z, CORES = 4, 8, 8, 2
SIDES = 2
AXES = ("x", "step", "side", "z", "core")


def index_of(x, y, z, core):
    return ((x * Y + y) * Z + z) * CORES + core


def place(z, tokens, q):
    ahead = lax.rem(tokens - z + Z, Z)
    even = lax.rem(ahead, 2) == 0
    turn = jnp.where(ahead >= 4, jnp.where(even, 0, 3), jnp.where(even, 2, 1))
    first = 4 * lax.rem(z, 2)
    y = jnp.where((ahead < 2) | (ahead > 5), lax.rem(first + 7 - q, Y), first + q)
    return lax.rem(z // 2 + turn, X), y


def to_feature_owner():
    x, y, z, core = (a.ravel() for a in np.indices((X, Y, Z, CORES)))
    plane = 2 * x + y // 4
    ahead = (z - plane) % Z
    turn = np.array([2, 1, 2, 1, 0, 3, 0, 3])[ahead]
    target_y = np.where((ahead < 2) | (ahead > 5), (4 * (plane % 2) + 7 - y % 4) % Y, y)
    targets = index_of((plane // 2 + turn) % X, target_y, plane, core)
    return [(int(a), int(b)) for a, b in zip(index_of(x, y, z, core), targets)]


def slot(tokens, half, h):
    core = lax.axis_index("core")
    q = 2 * (core if half == 0 else 1 - core) + h
    x, y = place(lax.axis_index("z"), tokens, q)
    return x * SIDES + lax.rem(y, SIDES), y // SIDES


def grad_of(grad_ref, tokens, half):
    blocks = [jnp.concatenate([grad_ref[slot(t, half, h)] for h in range(2)], axis=1) for t in tokens]
    return jnp.concatenate(blocks, axis=0)


def kernel_call(kernel, out_shape, flops, size, vmem=24, **more):
    return pl.pallas_call(
        kernel,
        out_shape=out_shape,
        compiler_params=pltpu.CompilerParams(vmem_limit_bytes=vmem * 1024 * 1024),
        cost_estimate=pl.CostEstimate(flops=flops, bytes_accessed=size, transcendentals=0),
        **more,
    )


def streamed_call(kernel, out_shape, flops, size, scratch_shapes):
    in_hbm = pl.BlockSpec(memory_space=pl.ANY)

    def call(*arrays):
        return kernel_call(
            kernel,
            out_shape,
            flops,
            size,
            vmem=60,
            in_specs=[in_hbm] * len(arrays),
            out_specs=jax.tree.map(lambda _: in_hbm, out_shape),
            scratch_shapes=scratch_shapes,
        )(*arrays)

    return call


def started(source, target, sem):
    copy = pltpu.make_async_copy(source, target, sem)
    copy.start()
    return copy


def hidden_kernel(gate_ref, up_ref, hidden_ref, gate_in, up_in, hidden_out, sems):
    parts = 2
    rows = gate_ref.shape[0] // parts
    spans = [pl.ds(i * rows, rows) for i in range(parts)]
    copies = [
        (started(gate_ref.at[r], gate_in.at[r], sems.at[2 * i]), started(up_ref.at[r], up_in.at[r], sems.at[2 * i + 1]))
        for i, r in enumerate(spans)
    ]
    stores = []
    for i, r in enumerate(spans):
        for copy in copies[i]:
            copy.wait()
        gate = gate_in[r].astype(jnp.float32)
        up = up_in[r].astype(jnp.float32)
        hidden_out[r] = (gate * jax.nn.sigmoid(gate) * up).astype(jnp.bfloat16)
        stores.append(started(hidden_out.at[r], hidden_ref.at[r], sems.at[2 * parts + i]))
    for store in stores:
        store.wait()


def share_kernel(grad_ref, own_ref, other_ref, share_ref, mine_ref, share_out, sems):
    weights = jnp.concatenate([own_ref[...], other_ref[...]], axis=1)
    tokens = mine_ref.shape[0]
    here = lax.axis_index("z")
    parts, copies = 2, []
    count = Z // parts

    def product(blocks):
        grad = jnp.concatenate([grad_of(grad_ref, blocks, half) for half in range(2)], axis=1)
        return lax.dot_general(grad, weights, (((1,), (1,)), ((), ())), preferred_element_type=jnp.float32)

    for i in range(parts):
        z = pl.ds(i * count, count)
        rows = product(range(i * count, (i + 1) * count))
        share_out[z] = rows.astype(jnp.bfloat16).reshape(count, tokens, -1)

        @pl.when(here // count == i)
        def _():
            share_out[here] = jnp.zeros(mine_ref.shape, jnp.bfloat16)

        copies.append(started(share_out.at[z], share_ref.at[z], sems.at[i]))
    mine_ref[...] = product([here])
    for copy in copies:
        copy.wait()


def output_kernel(hidden_ref, own_ref, other_ref, out_ref):
    _, _, tokens, sub = out_ref.shape
    for half, weights in enumerate((own_ref, other_ref)):
        product = jnp.dot(hidden_ref[...], weights[...], preferred_element_type=jnp.float32).astype(jnp.bfloat16)
        for z in range(Z):
            for h in range(2):
                out_ref[slot(z, half, h)] = product[z * tokens : (z + 1) * tokens, h * sub : (h + 1) * sub]


def weight_grad_kernel(hidden_ref, grad_ref, own_ref, other_ref):
    for half, out_ref in enumerate((own_ref, other_ref)):
        out_ref[...] = lax.dot_general(
            hidden_ref[...],
            grad_of(grad_ref, range(Z), half),
            (((0,), (0,)), ((), ())),
            preferred_element_type=jnp.float32,
        ).astype(out_ref.dtype)


def sum_kernel(parts_ref, sum_ref):
    total = parts_ref[0].astype(jnp.float32)
    for i in range(1, parts_ref.shape[0]):
        total = total + parts_ref[i].astype(jnp.float32)
    sum_ref[...] = total.astype(jnp.bfloat16)


def add_kernel(a_ref, b_ref, sum_ref):
    sum_ref[...] = (a_ref[...] + b_ref[...]).astype(jnp.bfloat16)


def gradient_kernel(mine_ref, others_ref, gate_ref, up_ref, gate_grad_ref, up_grad_ref):
    hidden_grad = mine_ref[...] + others_ref[...].astype(jnp.float32)
    gate = gate_ref[...].astype(jnp.float32)
    up = up_ref[...].astype(jnp.float32)
    sigmoid = jax.nn.sigmoid(gate)
    gate_grad_ref[...] = (hidden_grad * up * sigmoid * (1.0 + gate * (1.0 - sigmoid))).astype(jnp.bfloat16)
    up_grad_ref[...] = (hidden_grad * gate * sigmoid).astype(jnp.bfloat16)


def body(gate_pre, up_pre, down_weight, out_grad):
    bf16, f32, shape = jnp.bfloat16, jnp.float32, jax.ShapeDtypeStruct
    there = to_feature_owner()
    back = [(b, a) for a, b in there]
    tokens, units = gate_pre.shape
    sub, features = out_grad.shape[1], down_weight.shape[1]
    rows = Z * tokens
    flops = 2 * rows * units * CORES * features
    swap = [(0, 1), (1, 0)]
    together = lax.optimization_barrier

    def exchanged(array, axis):
        return lax.all_to_all(array, axis, split_axis=0, concat_axis=0, tiled=True)

    block = (tokens, units)
    vmem, dma = pltpu.VMEM, pltpu.SemaphoreType.DMA
    hidden = streamed_call(
        hidden_kernel, shape(block, bf16), 0, 6 * tokens * units, [vmem(block, bf16)] * 3 + [dma((6,))]
    )(gate_pre, up_pre)
    hidden, out_grad = together((hidden, out_grad))
    hidden_all = lax.all_gather(hidden, "z", axis=0, tiled=True)

    grad = lax.ppermute(out_grad, AXES, there)
    other_weight = lax.ppermute(down_weight, "core", swap)
    steps = Y // SIDES
    grad = exchanged(jnp.broadcast_to(grad, (steps, tokens, sub)), "step")
    grad = exchanged(jnp.broadcast_to(grad, (X * SIDES, steps, tokens, sub)), ("x", "side"))

    share, mine = kernel_call(
        share_kernel,
        (shape((Z, tokens, units), bf16), shape(block, f32)),
        flops,
        4 * rows * units,
        out_specs=(pl.BlockSpec(memory_space=pl.ANY), pl.BlockSpec(memory_space=pltpu.VMEM)),
        scratch_shapes=[vmem((Z, tokens, units), bf16), dma((2,))],
    )(grad, down_weight, other_weight)
    hidden_all, _ = together((hidden_all, mine))
    output = kernel_call(output_kernel, shape((X * SIDES, steps, tokens, sub), bf16), flops, 4 * rows * units)(
        hidden_all, down_weight, other_weight
    )

    others = lax.psum_scatter(share.reshape(rows, units), "z", scatter_dimension=0, tiled=True)
    gate_grad, up_grad = kernel_call(gradient_kernel, (shape(block, bf16),) * 2, 0, 14 * tokens * units)(
        mine, others, gate_pre, up_pre
    )

    output = exchanged(output, ("x", "side"))
    output = kernel_call(sum_kernel, shape((steps, tokens, sub), bf16), 0, 10 * rows * sub)(output)
    output = exchanged(output, "step")
    output = kernel_call(sum_kernel, shape((tokens, sub), bf16), 0, 10 * tokens * sub)(output)
    output = lax.ppermute(output, AXES, back)
    output, gate_grad, up_grad = together((output, gate_grad, up_grad))

    own, other = kernel_call(
        weight_grad_kernel, (shape((units, features), f32),) * 2, flops, 4 * rows * units
    )(hidden_all, grad)
    weight_grad = kernel_call(add_kernel, shape((units, features), bf16), 0, 10 * units * features)(
        own, lax.ppermute(other, "core", swap)
    )
    return output, gate_grad, up_grad, weight_grad


def solution(mesh):
    chips = Mesh(mesh.devices.reshape(X, Y // SIDES, SIDES, Z, CORES), AXES)
    by_token = P(("z", "core"), ("x", "step", "side"))
    by_unit = P(("x", "step", "side"), ("z", "core"))
    return jax.shard_map(
        body,
        mesh=chips,
        in_specs=(by_token, by_token, by_unit, by_token),
        out_specs=(by_token, by_token, by_token, by_unit),
        check_vma=False,
    )
```
